32 devices in a mesh: groups: 2 (over x), tp: 16 (over z, y, core).
Axes of the slice: x: 2, y: 2, z: 4, core: 2. Of those that a mesh axis runs over, the one named last changes fastest.
Arguments:
- tokens: bfloat16 [64, 8192], P(('groups', 'tp')), parts along dimension 0, may hold values from -6 to 6
- norm_gain_vector: float32 [8192], replicated, may hold values from 0.1 to 1.9
- query_weight: bfloat16 [8192, 2048], P(None, 'tp'), may hold values from -0.0625 to 0.0625
- key_value_weight: bfloat16 [8192, 2048], P(None, 'tp'), may hold values from -0.0625 to 0.0625
- output_weight: bfloat16 [2048, 8192], P('tp'), may hold values from -0.125 to 0.125
- adapter_down_factor: bfloat16 [32, 8192, 64], P(('groups', 'tp')), parts along dimension 0, may hold values from -0.0625 to 0.0625
- adapter_up_factor: bfloat16 [32, 64, 2048], P(('groups', 'tp')), parts along dimension 0, may hold values from -0.75 to 0.75
- cached_key_rows: bfloat16 [64, 128, 1024], P(('groups', 'tp')), parts along dimension 0, may hold values from -100 to 100
- cached_value_rows: bfloat16 [64, 128, 1024], P(('groups', 'tp')), parts along dimension 0, may hold values from -6 to 6
- row_adapter_index: int32 [64], P('groups'), parts along dimension 0, may hold values from 0 to 15
- cached_length_rows: int32 [64], P(('groups', 'tp')), parts along dimension 0, may hold values from 1 to 128, as said below
- adapter_slot_index: int32 [32], P('groups'), parts along dimension 0, may hold values from 0 to 15, each once
Outputs:
- attn_out: bfloat16 [64, 8192], P(('groups', 'tp')), parts along dimension 0
The draws below stay inside these ranges and needn't reach their ends.
There are 2 independent parts, one for each index of `groups`. The reference program is written for one: setup_inputs(seed, part) draws one part's arguments, and reference() takes and returns one part's arrays. A program takes and returns all parts, laid end to end along the dimension named above; an argument that names none is the same for every part. Nothing has to cross between parts.
Inputs may be any that keep to these rules, and one draw needn't show every extreme that they name: Each slot appears once; adapter a is stored at index adapter_slot_index[a] of adapter_down_factor and adapter_up_factor. `cached_length_rows`: some row has exactly 128 cached positions.
All inputs are finite; a program needn't handle non-finite values.
Results may differ from the reference program's by a relative error of at most 0.0085.
The reference program's roundings to bfloat16 on the way count: a program that leaves them out, or rounds other values in their place, can miss the bound.
Values may be sent and summed in bfloat16 or wider, within the bound.
A program may use at most 64 MiB of HBM per device.

```python
import math
import jax
import jax.numpy as jnp
import numpy as np
from jax import lax

MODEL_DIM = 8192
QUERY_HEADS = 16
KV_HEADS = 8
HEAD_WIDTH = 128
ADAPTER_RANK = 64
CACHE = 128
ROWS = 32
ADAPTER_TOTAL = 16


def draw_cached_key_rows(key, part):
    key = jax.random.fold_in(key, 11)
    first_key = jax.random.fold_in(key, 0)
    shape_all = (ROWS, CACHE, KV_HEADS * HEAD_WIDTH)
    return jnp.clip(jax.random.normal(first_key, shape_all, jnp.float32), -6.0, 6.0).astype(jnp.bfloat16)


def draw_cached_length_rows(key, part):
    key = jax.random.fold_in(key, 7)
    first_key, second_key = jax.random.split(key)
    lengths_all = jax.random.randint(first_key, (ROWS,), 1, CACHE + 1)
    chosen = jax.random.randint(second_key, (), 0, ROWS)
    return jnp.where(jnp.arange(ROWS) == chosen, CACHE, lengths_all).astype(jnp.int32)


def with_ends(drawn, own_key, smallest, top_value):
    extent = drawn.shape
    place = [jax.random.randint(jax.random.fold_in(own_key, axis), (), 0, extent[axis]) for axis in range(len(extent))]
    drawn = drawn.at[tuple(place)].set(smallest)
    longest = extent.index(max(extent))
    place[longest] = (place[longest] + 1) % extent[longest]
    return drawn.at[tuple(place)].set(top_value)


def steps_of(own_key, dims, pieces, smallest, high):
    level = 1.0
    for position, parts in pieces:
        steps = jax.random.uniform(jax.random.fold_in(jax.random.fold_in(own_key, 6), position), (parts,), jnp.float32, smallest / len(pieces), high / len(pieces))
        level = level * jnp.repeat(jnp.exp(steps), dims[position] // parts).reshape((-1,) + (1,) * (len(dims) - 1 - position))
    return level


def rank_bounds(number_of, lean):
    loads = [(1 << 20) // math.isqrt(rank ** lean) + 1 for rank in range(1, number_of + 1)]
    scale = 1 + sum(loads) // (1 << 30)
    return np.cumsum(np.array([max(1, weight // scale) for weight in loads]))


def ranked_ids(rng, shape, count, skew):
    grid = rank_bounds(count, skew)
    lot = jax.random.randint(jax.random.fold_in(rng, 1), shape, 0, int(grid[count - 1]))
    rank = jnp.searchsorted(jnp.asarray(grid, jnp.int32), lot, side="right")
    return jax.random.permutation(jax.random.fold_in(rng, 2), count)[rank].astype(jnp.int32)


def scatter_about(own_key, dims, deviation, limit, shards=(), kind=jnp.bfloat16):
    array = deviation * jax.random.normal(own_key, dims, jnp.float32)
    if shards:
        array = array * steps_of(own_key, dims, shards, -0.22, 0.18)
    return jnp.clip(array, -limit, limit).astype(kind)


def setup_inputs(seed: int = 0, part: int = 0) -> dict:
    arg_keys = jax.random.split(jax.random.key(seed), 13)
    own_keys = jax.random.split(jax.random.fold_in(arg_keys[12], part), 13)
    return {
        "tokens": scatter_about(own_keys[0], (ROWS, MODEL_DIM), 1.0, 6.0, ((0, 16),)),
        "norm_gain_vector": jnp.clip(1.0 + 0.18 * jax.random.normal(arg_keys[1], (MODEL_DIM,), jnp.float32), 0.1, 1.9),
        "query_weight": scatter_about(arg_keys[2], (MODEL_DIM, QUERY_HEADS * HEAD_WIDTH), MODEL_DIM ** -0.5, 0.0625, ((1, 16),)),
        "key_value_weight": scatter_about(arg_keys[3], (MODEL_DIM, 2 * KV_HEADS * HEAD_WIDTH), MODEL_DIM ** -0.5, 0.0625, ((1, 16),)),
        "output_weight": scatter_about(arg_keys[4], (QUERY_HEADS * HEAD_WIDTH, MODEL_DIM), (QUERY_HEADS * HEAD_WIDTH) ** -0.5, 0.125, ((0, 16),)),
        "adapter_down_factor": scatter_about(own_keys[5], (ADAPTER_TOTAL, MODEL_DIM, ADAPTER_RANK), MODEL_DIM ** -0.5, 0.0625, ((0, 16),)),
        "adapter_up_factor": scatter_about(own_keys[6], (ADAPTER_TOTAL, ADAPTER_RANK, QUERY_HEADS * HEAD_WIDTH), ADAPTER_RANK ** -0.5, 0.75, ((0, 16),)),
        "cached_key_rows": draw_cached_key_rows(jax.random.fold_in(jax.random.fold_in(arg_keys[12], part), 71), part),
        "cached_value_rows": scatter_about(own_keys[8], (ROWS, CACHE, KV_HEADS * HEAD_WIDTH), 1.0, 6.0, ((0, 16),)),
        "row_adapter_index": with_ends(ranked_ids(own_keys[9], (ROWS,), ADAPTER_TOTAL, 2), jax.random.fold_in(own_keys[9], 3), 0, ADAPTER_TOTAL - 1).astype(jnp.int32),
        "cached_length_rows": draw_cached_length_rows(jax.random.fold_in(jax.random.fold_in(arg_keys[12], part), 71), part),
        "adapter_slot_index": jax.random.permutation(own_keys[11], ADAPTER_TOTAL).astype(jnp.int32),
    }


EPSILON = 1e-05
ADAPTER_SCALE = 0.5
ROPE_BASE = 500000.0

def rotate(values_in, places):
    half_size = HEAD_WIDTH // 2
    freqs = ROPE_BASE ** (-jnp.arange(half_size, dtype=jnp.float32) / half_size)
    angles = places.astype(jnp.float32)[:, None, None] * freqs[None, None, :]
    cosine = jnp.cos(angles)
    sine = jnp.sin(angles)
    first_half = values_in[..., :half_size]
    second_half = values_in[..., half_size:]
    return jnp.concatenate([first_half * cosine - second_half * sine, second_half * cosine + first_half * sine], axis=-1)

def attend(query_vector, keyval, cached_key_rows, cached_value_rows, lengths_here):
    row_count = query_vector.shape[0]
    head_count = query_vector.shape[1] // HEAD_WIDTH
    group_size = head_count // KV_HEADS
    kv_width = KV_HEADS * HEAD_WIDTH
    queries = rotate(query_vector.astype(jnp.float32).reshape(row_count, head_count, HEAD_WIDTH), lengths_here).astype(jnp.bfloat16)
    new_keys = rotate(keyval[:, :kv_width].astype(jnp.float32).reshape(row_count, KV_HEADS, HEAD_WIDTH), lengths_here).astype(jnp.bfloat16)
    new_values = keyval[:, kv_width:].reshape(row_count, KV_HEADS, HEAD_WIDTH)
    grouped = queries.reshape(row_count, KV_HEADS, group_size, HEAD_WIDTH).astype(jnp.float32)
    old_keys = cached_key_rows.reshape(row_count, -1, KV_HEADS, HEAD_WIDTH).astype(jnp.float32)
    old_values = cached_value_rows.reshape(row_count, -1, KV_HEADS, HEAD_WIDTH).astype(jnp.float32)
    factor = 1.0 / math.sqrt(HEAD_WIDTH)
    scores = jnp.einsum('rgqd,rcgd->rgqc', grouped, old_keys) * factor
    own_score = jnp.einsum('rgqd,rgd->rgq', grouped, new_keys.astype(jnp.float32)) * factor
    valid = jnp.arange(old_keys.shape[1], dtype=jnp.int32)[None, :] < lengths_here[:, None]
    scores = jnp.where(valid[:, None, None, :], scores, -jnp.inf)
    highest = jnp.maximum(lax.optimization_barrier(jnp.max(scores, axis=-1)), own_score)
    expos = jnp.exp(scores - highest[..., None])
    own_expo = jnp.exp(own_score - highest)
    total = lax.optimization_barrier(jnp.sum(expos, axis=-1)) + own_expo
    weights = (expos / total[..., None]).astype(jnp.bfloat16)
    own_weight = (own_expo / total).astype(jnp.bfloat16)
    context = jnp.einsum('rgqc,rcgd->rgqd', weights.astype(jnp.float32), old_values)
    context = context + own_weight.astype(jnp.float32)[..., None] * new_values.astype(jnp.float32)[:, :, None, :]
    return context.astype(jnp.bfloat16).reshape(row_count, head_count * HEAD_WIDTH)

def reference(tokens, norm_gain_vector, query_weight, key_value_weight, output_weight, adapter_down_factor, adapter_up_factor, cached_key_rows, cached_value_rows, row_adapter_index, cached_length_rows, adapter_slot_index):
    widened = tokens.astype(jnp.float32)
    normalized_input = (widened * lax.rsqrt(lax.optimization_barrier(jnp.mean(widened * widened, axis=-1, keepdims=True)) + EPSILON) * norm_gain_vector).astype(jnp.bfloat16)
    table = row_adapter_index[:, None] == jnp.arange(ADAPTER_TOTAL, dtype=jnp.int32)[None, :]
    slot = lax.optimization_barrier(jnp.sum(jnp.where(table, adapter_slot_index[None, :], 0), axis=1)).astype(jnp.int32)
    picked = slot[:, None] == jnp.arange(ADAPTER_TOTAL, dtype=jnp.int32)[None, :]
    down_factor_rows = jnp.transpose(adapter_down_factor, (1, 0, 2)).reshape(MODEL_DIM, ADAPTER_TOTAL * ADAPTER_RANK)
    every_low = jnp.dot(normalized_input, down_factor_rows, preferred_element_type=jnp.float32).reshape(ROWS, ADAPTER_TOTAL, ADAPTER_RANK)
    low = lax.optimization_barrier(jnp.sum(jnp.where(picked[:, :, None], every_low, 0.0), axis=1)).astype(jnp.bfloat16)
    rank_activation = jnp.where(picked[:, :, None], low[:, None, :], jnp.zeros((), jnp.bfloat16)).reshape(ROWS, ADAPTER_TOTAL * ADAPTER_RANK)
    query_correction = jnp.dot(rank_activation, adapter_up_factor.reshape(ADAPTER_TOTAL * ADAPTER_RANK, QUERY_HEADS * HEAD_WIDTH), preferred_element_type=jnp.float32)
    query_vector = (jnp.dot(normalized_input, query_weight, preferred_element_type=jnp.float32) + ADAPTER_SCALE * query_correction).astype(jnp.bfloat16)
    keyval = jnp.dot(normalized_input, key_value_weight, preferred_element_type=jnp.float32).astype(jnp.bfloat16)
    context = attend(query_vector, keyval, cached_key_rows, cached_value_rows, cached_length_rows)
    return jnp.dot(context, output_weight, preferred_element_type=jnp.float32).astype(jnp.bfloat16)
```

```python
import functools
import math

import jax
import jax.numpy as jnp
from jax import lax
from jax.experimental import pallas as pl
from jax.experimental.pallas import tpu as pltpu
from jax.sharding import PartitionSpec as P

KV_HEADS = 8
HEAD_WIDTH = 128


EPSILON = 1e-05
ADAPTER_SCALE = 0.5
ROPE_BASE = 500000.0

VMEM_LIMIT = 24 * 1024 * 1024
CHUNKS = 4
FOLD = 8


def peers(n):
    me = lax.axis_index("tp")
    outer = n // 4
    a, b, c = me // 4, (me // 2) % 2, me % 2
    core_peer = a * 4 + b * 2 + (1 - c)
    mid_peer = a * 4 + (1 - b) * 2 + c
    ahead = [((a + k) % outer) * 4 + b * 2 + c for k in range(outer)]
    behind = [((a + outer - k) % outer) * 4 + b * 2 + c for k in range(outer)]
    return me, outer, a, b, c, core_peer, mid_peer, ahead, behind


def greet(partners):
    barrier = pltpu.get_barrier_semaphore()
    for partner in partners:
        pl.semaphore_signal(
            barrier, inc=1, device_id={"tp": partner}, device_id_type=pl.DeviceIdType.MESH
        )
    pl.semaphore_wait(barrier, len(partners))


def send(src, dst, send_sem, recv_sem, target):
    return pltpu.make_async_remote_copy(
        src_ref=src,
        dst_ref=dst,
        send_sem=send_sem,
        recv_sem=recv_sem,
        device_id={"tp": target},
        device_id_type=pl.DeviceIdType.MESH,
    )


def gather_kernel(n, width, x_ref, gain_ref, out_ref, far_send, mid_send, core_send, recv):
    me, outer, a, b, c, core_peer, mid_peer, ahead, behind = peers(n)
    rows = x_ref.shape[0] // FOLD
    for r in range(rows):
        part = pl.ds(r * FOLD, FOLD)
        x = x_ref[part, :].astype(jnp.float32)
        mean = jnp.sum(x * x) / width
        out_ref[me, part, :] = (x * lax.rsqrt(mean + EPSILON) * gain_ref[...]).astype(jnp.bfloat16)
    greet([core_peer, mid_peer] + ahead[1:])

    def push(block, sem, target):
        copy = send(out_ref.at[block], out_ref.at[block], sem, recv.at[block], target)
        copy.start()
        return copy

    def arrived(block):
        send(out_ref.at[block], out_ref.at[block], core_send.at[0], recv.at[block], core_peer).wait_recv()

    copies = [push(me, far_send.at[k], ahead[k]) for k in range(1, outer)]
    copies.append(push(me, mid_send.at[0], mid_peer))
    copies.append(push(me, core_send.at[0], core_peer))
    for k in range(1, outer):
        arrived(behind[k])
        copies.append(push(behind[k], mid_send.at[k], mid_peer))
        copies.append(push(behind[k], core_send.at[k], core_peer))
    across = [behind[k] - b * 2 + (1 - b) * 2 for k in range(outer)]
    for k in range(outer):
        arrived(across[k])
        copies.append(push(across[k], core_send.at[outer + k], core_peer))
    for k in range(outer):
        arrived(behind[k] - c + (1 - c))
    for k in range(outer):
        arrived(across[k] - c + (1 - c))
    for copy in copies:
        copy.wait_send()


def normalize_and_gather(tokens, gain, n):
    rows, width = tokens.shape
    fold_width = width // FOLD
    outer = n // 4
    gathered = pl.pallas_call(
        functools.partial(gather_kernel, n, width),
        out_shape=jax.ShapeDtypeStruct((n, rows * FOLD, fold_width), jnp.bfloat16),
        in_specs=[pl.BlockSpec(memory_space=pltpu.VMEM)] * 2,
        out_specs=pl.BlockSpec(memory_space=pltpu.VMEM),
        scratch_shapes=[
            pltpu.SemaphoreType.DMA((outer,)),
            pltpu.SemaphoreType.DMA((outer,)),
            pltpu.SemaphoreType.DMA((2 * outer,)),
            pltpu.SemaphoreType.DMA((n,)),
        ],
        compiler_params=pltpu.CompilerParams(
            collective_id=0, has_side_effects=True, vmem_limit_bytes=VMEM_LIMIT
        ),
    )(tokens.reshape(rows * FOLD, fold_width), gain.reshape(FOLD, fold_width))
    return gathered.reshape(n * rows, width)


def project_kernel(
    n, rows, ctx_ref, w_ref, out_ref, p_ref, r1, r2, x_ref, r3, s1, q1, s2, q2, s3, q3
):
    me, outer, a, b, c, core_peer, mid_peer, ahead, behind = peers(n)
    cols = w_ref.shape[1] // CHUNKS
    quarter = outer * rows
    greet([core_peer, mid_peer] + ahead[1:])
    first, second, third = [], [], []
    for i in range(CHUNKS):
        part = jnp.dot(
            ctx_ref[...], w_ref[:, i * cols : (i + 1) * cols], preferred_element_type=jnp.float32
        )
        p_ref[i] = part.reshape(2, 2, quarter, cols)
        copy = send(p_ref.at[i, 1 - c], r1.at[i], s1.at[i], q1.at[i], core_peer)
        copy.start()
        first.append(copy)
    for i in range(CHUNKS):
        first[i].wait()
        p_ref[i, c] = p_ref[i, c] + r1[i]
        copy = send(p_ref.at[i, c, 1 - b], r2.at[i], s2.at[i], q2.at[i], mid_peer)
        copy.start()
        second.append(copy)
    for i in range(CHUNKS):
        second[i].wait()
        both = p_ref[i, c, b] + r2[i]
        for t in range(outer):
            x_ref[i, t] = both[t * rows : (t + 1) * rows, :]
        group = []
        for k in range(1, outer):
            copy = send(
                x_ref.at[i, (a + k) % outer], r3.at[i, k], s3.at[i, k], q3.at[i, k], ahead[k]
            )
            copy.start()
            group.append(copy)
        third.append(group)
    for i in range(CHUNKS):
        total = x_ref[i, a]
        for k in range(1, outer):
            third[i][k - 1].wait()
            total = total + r3[i, k]
        out_ref[:, i * cols : (i + 1) * cols] = total.astype(jnp.bfloat16)


def project_and_scatter(head_context, weight, n):
    total_rows, depth = head_context.shape
    rows = total_rows // n
    outer = n // 4
    width = weight.shape[1]
    cols = width // CHUNKS
    quarter = outer * rows
    ordered = jnp.transpose(head_context.reshape(outer, 2, 2, rows, depth), (2, 1, 0, 3, 4))
    return pl.pallas_call(
        functools.partial(project_kernel, n, rows),
        out_shape=jax.ShapeDtypeStruct((rows, width), jnp.bfloat16),
        in_specs=[pl.BlockSpec(memory_space=pltpu.VMEM)] * 2,
        out_specs=pl.BlockSpec(memory_space=pltpu.VMEM),
        scratch_shapes=[
            pltpu.VMEM((CHUNKS, 2, 2, quarter, cols), jnp.float32),
            pltpu.VMEM((CHUNKS, 2, quarter, cols), jnp.float32),
            pltpu.VMEM((CHUNKS, quarter, cols), jnp.float32),
            pltpu.VMEM((CHUNKS, outer, rows, cols), jnp.float32),
            pltpu.VMEM((CHUNKS, outer, rows, cols), jnp.float32),
            pltpu.SemaphoreType.DMA((CHUNKS,)),
            pltpu.SemaphoreType.DMA((CHUNKS,)),
            pltpu.SemaphoreType.DMA((CHUNKS,)),
            pltpu.SemaphoreType.DMA((CHUNKS,)),
            pltpu.SemaphoreType.DMA((CHUNKS, outer)),
            pltpu.SemaphoreType.DMA((CHUNKS, outer)),
        ],
        compiler_params=pltpu.CompilerParams(
            collective_id=1, has_side_effects=True, vmem_limit_bytes=VMEM_LIMIT
        ),
    )(ordered.reshape(total_rows, depth), weight)


def rotate(values_in, places):
    half_size = HEAD_WIDTH // 2
    freqs = ROPE_BASE ** (-jnp.arange(half_size, dtype=jnp.float32) / half_size)
    angles = places.astype(jnp.float32)[:, None, None] * freqs[None, None, :]
    cosine = jnp.cos(angles)
    sine = jnp.sin(angles)
    first_half = values_in[..., :half_size]
    second_half = values_in[..., half_size:]
    return jnp.concatenate(
        [first_half * cosine - second_half * sine, second_half * cosine + first_half * sine],
        axis=-1,
    )


def attend(query_vector, keyval, cached_key_rows, cached_value_rows, lengths_here):
    row_count = query_vector.shape[0]
    head_count = query_vector.shape[1] // HEAD_WIDTH
    group_size = head_count // KV_HEADS
    kv_width = KV_HEADS * HEAD_WIDTH
    queries = rotate(
        query_vector.astype(jnp.float32).reshape(row_count, head_count, HEAD_WIDTH), lengths_here
    ).astype(jnp.bfloat16)
    new_keys = rotate(
        keyval[:, :kv_width].astype(jnp.float32).reshape(row_count, KV_HEADS, HEAD_WIDTH),
        lengths_here,
    ).astype(jnp.bfloat16)
    new_values = keyval[:, kv_width:].reshape(row_count, KV_HEADS, HEAD_WIDTH)
    grouped = queries.reshape(row_count, KV_HEADS, group_size, HEAD_WIDTH)
    old_keys = cached_key_rows.reshape(row_count, -1, KV_HEADS, HEAD_WIDTH)
    old_values = cached_value_rows.reshape(row_count, -1, KV_HEADS, HEAD_WIDTH)
    factor = 1.0 / math.sqrt(HEAD_WIDTH)
    scores = (
        jnp.einsum("rgqd,rcgd->rgqc", grouped, old_keys, preferred_element_type=jnp.float32)
        * factor
    )
    own_score = (
        jnp.einsum("rgqd,rgd->rgq", grouped, new_keys, preferred_element_type=jnp.float32) * factor
    )
    valid = jnp.arange(old_keys.shape[1], dtype=jnp.int32)[None, :] < lengths_here[:, None]
    scores = jnp.where(valid[:, None, None, :], scores, -jnp.inf)
    highest = jnp.maximum(jnp.max(scores, axis=-1), own_score)
    expos = jnp.exp(scores - highest[..., None])
    own_expo = jnp.exp(own_score - highest)
    total = jnp.sum(expos, axis=-1) + own_expo
    weights = (expos / total[..., None]).astype(jnp.bfloat16)
    own_weight = (own_expo / total).astype(jnp.bfloat16)
    context = jnp.einsum("rgqc,rcgd->rgqd", weights, old_values, preferred_element_type=jnp.float32)
    context = (
        context
        + own_weight.astype(jnp.float32)[..., None] * new_values.astype(jnp.float32)[:, :, None, :]
    )
    return context.astype(jnp.bfloat16).reshape(row_count, head_count * HEAD_WIDTH)


def on_device(
    tokens,
    norm_gain_vector,
    query_weight,
    key_value_weight,
    output_weight,
    adapter_down_factor,
    adapter_up_factor,
    cached_key_rows,
    cached_value_rows,
    row_adapter_index,
    cached_length_rows,
    adapter_slot_index,
):
    position = lax.axis_index("tp")
    tp = lax.axis_size("tp")
    adapter_count = adapter_slot_index.shape[0]
    resident_count = adapter_down_factor.shape[0]
    rank_width = adapter_down_factor.shape[2]
    hidden_width = adapter_down_factor.shape[1]
    table = row_adapter_index[:, None] == jnp.arange(adapter_count, dtype=jnp.int32)[None, :]
    slot = jnp.sum(jnp.where(table, adapter_slot_index[None, :], 0), axis=1)
    local_slots = position * resident_count + jnp.arange(resident_count, dtype=jnp.int32)
    owned = slot[:, None] == local_slots[None, :]
    down_factor_rows = jnp.transpose(adapter_down_factor, (1, 0, 2)).reshape(
        hidden_width, resident_count * rank_width
    )
    query_cols = query_weight.shape[1]
    kv_cols = key_value_weight.shape[1]
    piece = normalize_and_gather(tokens, norm_gain_vector, tp)
    piece_rows = piece.shape[0]
    query_part = jnp.dot(piece, query_weight, preferred_element_type=jnp.float32)
    kv_part = jnp.dot(piece, key_value_weight, preferred_element_type=jnp.float32)
    low_part = jnp.dot(piece, down_factor_rows, preferred_element_type=jnp.float32).reshape(
        piece_rows, resident_count, rank_width
    )
    low = low_part.astype(jnp.bfloat16)
    masked_low = jnp.where(owned[:, :, None], low, jnp.zeros((), jnp.bfloat16)).reshape(
        piece_rows, resident_count * rank_width
    )
    up_factor_rows = adapter_up_factor.reshape(
        resident_count * rank_width, adapter_up_factor.shape[2]
    )
    terms = jnp.dot(masked_low, up_factor_rows, preferred_element_type=jnp.float32)
    packed = jnp.concatenate([query_part, kv_part, terms], axis=1)
    packed = packed.reshape(tp, piece_rows // tp, packed.shape[1])
    received = lax.all_to_all(packed, "tp", split_axis=0, concat_axis=0, tiled=True)
    own_rows = piece_rows // tp
    plain_query = jnp.transpose(received[:, :, :query_cols], (1, 0, 2)).reshape(own_rows, -1)
    row_keyval = (
        jnp.transpose(received[:, :, query_cols : query_cols + kv_cols], (1, 0, 2))
        .reshape(own_rows, -1)
    )
    row_keyval = lax.reduce_precision(row_keyval, 8, 7).astype(jnp.bfloat16)
    correction = jnp.sum(received[:, :, query_cols + kv_cols :], axis=0)
    row_query = lax.reduce_precision(plain_query + ADAPTER_SCALE * correction, 8, 7).astype(
        jnp.bfloat16
    )
    context = attend(row_query, row_keyval, cached_key_rows, cached_value_rows, cached_length_rows)
    head_context = lax.all_to_all(context, "tp", split_axis=1, concat_axis=0, tiled=True)
    return project_and_scatter(head_context, output_weight, tp)


def solution(mesh):
    in_specs = (
        P(("groups", "tp"), None),
        P(),
        P(None, "tp"),
        P(None, "tp"),
        P("tp", None),
        P(("groups", "tp"), None, None),
        P(("groups", "tp"), None, None),
        P(("groups", "tp"), None, None),
        P(("groups", "tp"), None, None),
        P("groups"),
        P(("groups", "tp")),
        P("groups"),
    )
    out_specs = P(("groups", "tp"), None)
    return jax.shard_map(
        on_device, mesh=mesh, in_specs=in_specs, out_specs=out_specs, check_vma=False
    )
```

```python
import functools
import math

import jax
import jax.numpy as jnp
from jax import lax
from jax.experimental import pallas as pl
from jax.experimental.pallas import tpu as pltpu
from jax.sharding import PartitionSpec as P

KV_HEADS = 8
HEAD_WIDTH = 128


EPSILON = 1e-05
ADAPTER_SCALE = 0.5
ROPE_BASE = 500000.0

VMEM_LIMIT = 24 * 1024 * 1024
CHUNKS = 4
FOLD = 8


def peers(n):
    me = lax.axis_index("tp")
    outer = n // 4
    a, b, c = me // 4, (me // 2) % 2, me % 2
    core_peer = a * 4 + b * 2 + (1 - c)
    mid_peer = a * 4 + (1 - b) * 2 + c
    ahead = [((a + k) % outer) * 4 + b * 2 + c for k in range(outer)]
    behind = [((a + outer - k) % outer) * 4 + b * 2 + c for k in range(outer)]
    return me, outer, a, b, c, core_peer, mid_peer, ahead, behind


def greet(partners):
    barrier = pltpu.get_barrier_semaphore()
    for partner in partners:
        pl.semaphore_signal(
            barrier, inc=1, device_id={"tp": partner}, device_id_type=pl.DeviceIdType.MESH
        )
    pl.semaphore_wait(barrier, len(partners))


def send(src, dst, send_sem, recv_sem, target):
    return pltpu.make_async_remote_copy(
        src_ref=src,
        dst_ref=dst,
        send_sem=send_sem,
        recv_sem=recv_sem,
        device_id={"tp": target},
        device_id_type=pl.DeviceIdType.MESH,
    )


def gather_kernel(n, width, x_ref, gain_ref, out_ref, far_send, mid_send, core_send, recv):
    me, outer, a, b, c, core_peer, mid_peer, ahead, behind = peers(n)
    rows = x_ref.shape[0] // FOLD
    for r in range(rows):
        part = pl.ds(r * FOLD, FOLD)
        x = x_ref[part, :].astype(jnp.float32)
        mean = jnp.sum(x * x) / width
        out_ref[me, part, :] = (x * lax.rsqrt(mean + EPSILON) * gain_ref[...]).astype(jnp.bfloat16)
    greet([core_peer, mid_peer] + ahead[1:])

    def push(block, sem, target):
        copy = send(out_ref.at[block], out_ref.at[block], sem, recv.at[block], target)
        copy.start()
        return copy

    def arrived(block):
        send(out_ref.at[block], out_ref.at[block], core_send.at[0], recv.at[block], core_peer).wait_recv()

    copies = [push(me, far_send.at[k], ahead[k]) for k in range(1, outer)]
    copies.append(push(me, mid_send.at[0], mid_peer))
    copies.append(push(me, core_send.at[0], core_peer))
    for k in range(1, outer):
        arrived(behind[k])
        copies.append(push(behind[k], mid_send.at[k], mid_peer))
        copies.append(push(behind[k], core_send.at[k], core_peer))
    across = [behind[k] - b * 2 + (1 - b) * 2 for k in range(outer)]
    for k in range(outer):
        arrived(across[k])
        copies.append(push(across[k], core_send.at[outer + k], core_peer))
    for k in range(outer):
        arrived(behind[k] - c + (1 - c))
    for k in range(outer):
        arrived(across[k] - c + (1 - c))
    for copy in copies:
        copy.wait_send()


def normalize_and_gather(tokens, gain, n):
    rows, width = tokens.shape
    fold_width = width // FOLD
    outer = n // 4
    gathered = pl.pallas_call(
        functools.partial(gather_kernel, n, width),
        out_shape=jax.ShapeDtypeStruct((n, rows * FOLD, fold_width), jnp.bfloat16),
        in_specs=[pl.BlockSpec(memory_space=pltpu.VMEM)] * 2,
        out_specs=pl.BlockSpec(memory_space=pltpu.VMEM),
        scratch_shapes=[
            pltpu.SemaphoreType.DMA((outer,)),
            pltpu.SemaphoreType.DMA((outer,)),
            pltpu.SemaphoreType.DMA((2 * outer,)),
            pltpu.SemaphoreType.DMA((n,)),
        ],
        compiler_params=pltpu.CompilerParams(
            collective_id=0, has_side_effects=True, vmem_limit_bytes=VMEM_LIMIT
        ),
    )(tokens.reshape(rows * FOLD, fold_width), gain.reshape(FOLD, fold_width))
    return gathered.reshape(n * rows, width)


def others(n):
    me = lax.axis_index("tp")
    return me, [(me + k) % n for k in range(1, n)], [(me + n - k) % n for k in range(1, n)]


def exchange_kernel(n, packed_ref, out_ref, own_sem, send_sem, recv_sem):
    me, to, origin = others(n)
    own = pltpu.make_async_copy(packed_ref.at[me], out_ref.at[me], own_sem)
    own.start()
    greet(to)
    copies = []
    for k in range(n - 1):
        copy = send(
            packed_ref.at[to[k]], out_ref.at[me], send_sem.at[k], recv_sem.at[k], to[k]
        )
        copy.start()
        copies.append(copy)
    own.wait()
    for k in range(n - 1):
        copies[k].wait_send()
        send(
            packed_ref.at[to[k]], out_ref.at[origin[k]], send_sem.at[k], recv_sem.at[k], to[k]
        ).wait_recv()


def exchange(packed, n):
    return pl.pallas_call(
        functools.partial(exchange_kernel, n),
        out_shape=jax.ShapeDtypeStruct(packed.shape, packed.dtype),
        in_specs=[pl.BlockSpec(memory_space=pltpu.VMEM)],
        out_specs=pl.BlockSpec(memory_space=pltpu.VMEM),
        scratch_shapes=[
            pltpu.SemaphoreType.DMA(()),
            pltpu.SemaphoreType.DMA((n - 1,)),
            pltpu.SemaphoreType.DMA((n - 1,)),
        ],
        compiler_params=pltpu.CompilerParams(
            collective_id=2, has_side_effects=True, vmem_limit_bytes=VMEM_LIMIT
        ),
    )(packed)


def project_kernel(
    n,
    rows,
    heads_ref,
    w_ref,
    out_ref,
    h_ref,
    ctx_ref,
    p_ref,
    r1,
    r2,
    x_ref,
    r3,
    s0,
    q0,
    s1,
    q1,
    s2,
    q2,
    s3,
    q3,
):
    me, outer, a, b, c, core_peer, mid_peer, ahead, behind = peers(n)
    cols = w_ref.shape[1] // CHUNKS
    quarter = outer * rows
    slot = (c * 2 + b) * outer + a
    _, to, _ = others(n)
    greet(to)
    sent = []
    for k in range(n - 1):
        copy = send(heads_ref.at[to[k]], h_ref.at[slot], s0.at[k], q0.at[slot], to[k])
        copy.start()
        sent.append(copy)
    h_ref[slot] = heads_ref[me]
    for k in range(n - 1):
        source = (me + n - 1 - k) % n
        place = ((source % 2) * 2 + (source // 2) % 2) * outer + source // 4
        send(heads_ref.at[to[k]], h_ref.at[place], s0.at[k], q0.at[place], to[k]).wait_recv()
    for t in range(n):
        ctx_ref[t * rows : (t + 1) * rows, :] = h_ref[t]
    context = ctx_ref[...].astype(jnp.bfloat16)
    first, second, third = [], [], []
    for i in range(CHUNKS):
        part = jnp.dot(
            context, w_ref[:, i * cols : (i + 1) * cols], preferred_element_type=jnp.float32
        )
        p_ref[i] = part.reshape(2, 2, quarter, cols)
        copy = send(p_ref.at[i, 1 - c], r1.at[i], s1.at[i], q1.at[i], core_peer)
        copy.start()
        first.append(copy)
    for i in range(CHUNKS):
        first[i].wait()
        p_ref[i, c] = p_ref[i, c] + r1[i]
        copy = send(p_ref.at[i, c, 1 - b], r2.at[i], s2.at[i], q2.at[i], mid_peer)
        copy.start()
        second.append(copy)
    for i in range(CHUNKS):
        second[i].wait()
        both = p_ref[i, c, b] + r2[i]
        for t in range(outer):
            x_ref[i, t] = both[t * rows : (t + 1) * rows, :]
        group = []
        for k in range(1, outer):
            copy = send(
                x_ref.at[i, (a + k) % outer], r3.at[i, k], s3.at[i, k], q3.at[i, k], ahead[k]
            )
            copy.start()
            group.append(copy)
        third.append(group)
    for i in range(CHUNKS):
        total = x_ref[i, a]
        for k in range(1, outer):
            third[i][k - 1].wait()
            total = total + r3[i, k]
        out_ref[:, i * cols : (i + 1) * cols] = total.astype(jnp.bfloat16)
    for copy in sent:
        copy.wait_send()


def project_and_scatter(heads, weight, n):
    rows, depth = heads.shape[1:]
    outer = n // 4
    width = weight.shape[1]
    cols = width // CHUNKS
    quarter = outer * rows
    return pl.pallas_call(
        functools.partial(project_kernel, n, rows),
        out_shape=jax.ShapeDtypeStruct((rows, width), jnp.bfloat16),
        in_specs=[pl.BlockSpec(memory_space=pltpu.VMEM)] * 2,
        out_specs=pl.BlockSpec(memory_space=pltpu.VMEM),
        scratch_shapes=[
            pltpu.VMEM((n, rows, depth), jnp.float32),
            pltpu.VMEM((n * rows, depth), jnp.float32),
            pltpu.VMEM((CHUNKS, 2, 2, quarter, cols), jnp.float32),
            pltpu.VMEM((CHUNKS, 2, quarter, cols), jnp.float32),
            pltpu.VMEM((CHUNKS, quarter, cols), jnp.float32),
            pltpu.VMEM((CHUNKS, outer, rows, cols), jnp.float32),
            pltpu.VMEM((CHUNKS, outer, rows, cols), jnp.float32),
            pltpu.SemaphoreType.DMA((n,)),
            pltpu.SemaphoreType.DMA((n,)),
            pltpu.SemaphoreType.DMA((CHUNKS,)),
            pltpu.SemaphoreType.DMA((CHUNKS,)),
            pltpu.SemaphoreType.DMA((CHUNKS,)),
            pltpu.SemaphoreType.DMA((CHUNKS,)),
            pltpu.SemaphoreType.DMA((CHUNKS, outer)),
            pltpu.SemaphoreType.DMA((CHUNKS, outer)),
        ],
        compiler_params=pltpu.CompilerParams(
            collective_id=1, has_side_effects=True, vmem_limit_bytes=VMEM_LIMIT
        ),
    )(heads, weight)


def rotate(values_in, places):
    half_size = HEAD_WIDTH // 2
    freqs = ROPE_BASE ** (-jnp.arange(half_size, dtype=jnp.float32) / half_size)
    angles = places.astype(jnp.float32)[:, None, None] * freqs[None, None, :]
    cosine = jnp.cos(angles)
    sine = jnp.sin(angles)
    first_half = values_in[..., :half_size]
    second_half = values_in[..., half_size:]
    return jnp.concatenate(
        [first_half * cosine - second_half * sine, second_half * cosine + first_half * sine],
        axis=-1,
    )


def attend(query_vector, keyval, cached_key_rows, cached_value_rows, lengths_here):
    row_count = query_vector.shape[0]
    head_count = query_vector.shape[1] // HEAD_WIDTH
    group_size = head_count // KV_HEADS
    kv_width = KV_HEADS * HEAD_WIDTH
    queries = rotate(
        query_vector.astype(jnp.float32).reshape(row_count, head_count, HEAD_WIDTH), lengths_here
    ).astype(jnp.bfloat16)
    new_keys = rotate(
        keyval[:, :kv_width].astype(jnp.float32).reshape(row_count, KV_HEADS, HEAD_WIDTH),
        lengths_here,
    ).astype(jnp.bfloat16)
    new_values = keyval[:, kv_width:].reshape(row_count, KV_HEADS, HEAD_WIDTH)
    grouped = queries.reshape(row_count, KV_HEADS, group_size, HEAD_WIDTH)
    old_keys = cached_key_rows.reshape(row_count, -1, KV_HEADS, HEAD_WIDTH)
    old_values = cached_value_rows.reshape(row_count, -1, KV_HEADS, HEAD_WIDTH)
    factor = 1.0 / math.sqrt(HEAD_WIDTH)
    scores = (
        jnp.einsum("rgqd,rcgd->rgqc", grouped, old_keys, preferred_element_type=jnp.float32)
        * factor
    )
    own_score = (
        jnp.einsum("rgqd,rgd->rgq", grouped, new_keys, preferred_element_type=jnp.float32) * factor
    )
    valid = jnp.arange(old_keys.shape[1], dtype=jnp.int32)[None, :] < lengths_here[:, None]
    scores = jnp.where(valid[:, None, None, :], scores, -jnp.inf)
    highest = jnp.maximum(jnp.max(scores, axis=-1), own_score)
    expos = jnp.exp(scores - highest[..., None])
    own_expo = jnp.exp(own_score - highest)
    total = jnp.sum(expos, axis=-1) + own_expo
    weights = (expos / total[..., None]).astype(jnp.bfloat16)
    own_weight = (own_expo / total).astype(jnp.bfloat16)
    context = jnp.einsum("rgqc,rcgd->rgqd", weights, old_values, preferred_element_type=jnp.float32)
    context = (
        context
        + own_weight.astype(jnp.float32)[..., None] * new_values.astype(jnp.float32)[:, :, None, :]
    )
    return context.reshape(row_count, head_count * HEAD_WIDTH)


def on_device(
    tokens,
    norm_gain_vector,
    query_weight,
    key_value_weight,
    output_weight,
    adapter_down_factor,
    adapter_up_factor,
    cached_key_rows,
    cached_value_rows,
    row_adapter_index,
    cached_length_rows,
    adapter_slot_index,
):
    position = lax.axis_index("tp")
    tp = lax.axis_size("tp")
    adapter_count = adapter_slot_index.shape[0]
    resident_count = adapter_down_factor.shape[0]
    rank_width = adapter_down_factor.shape[2]
    hidden_width = adapter_down_factor.shape[1]
    table = row_adapter_index[:, None] == jnp.arange(adapter_count, dtype=jnp.int32)[None, :]
    slot = jnp.sum(jnp.where(table, adapter_slot_index[None, :], 0), axis=1)
    local_slots = position * resident_count + jnp.arange(resident_count, dtype=jnp.int32)
    owned = slot[:, None] == local_slots[None, :]
    down_factor_rows = jnp.transpose(adapter_down_factor, (1, 0, 2)).reshape(
        hidden_width, resident_count * rank_width
    )
    query_cols = query_weight.shape[1]
    kv_cols = key_value_weight.shape[1]
    piece = normalize_and_gather(tokens, norm_gain_vector, tp)
    piece_rows = piece.shape[0]
    query_part = jnp.dot(piece, query_weight, preferred_element_type=jnp.float32)
    kv_part = jnp.dot(piece, key_value_weight, preferred_element_type=jnp.float32)
    low_part = jnp.dot(piece, down_factor_rows, preferred_element_type=jnp.float32).reshape(
        piece_rows, resident_count, rank_width
    )
    low = low_part.astype(jnp.bfloat16)
    masked_low = jnp.where(owned[:, :, None], low, jnp.zeros((), jnp.bfloat16)).reshape(
        piece_rows, resident_count * rank_width
    )
    up_factor_rows = adapter_up_factor.reshape(
        resident_count * rank_width, adapter_up_factor.shape[2]
    )
    terms = jnp.dot(masked_low, up_factor_rows, preferred_element_type=jnp.float32)
    packed = jnp.concatenate([query_part, kv_part, terms], axis=1)
    packed = packed.reshape(tp, piece_rows // tp, packed.shape[1])
    received = exchange(packed, tp)
    own_rows = piece_rows // tp
    plain_query = jnp.transpose(received[:, :, :query_cols], (1, 0, 2)).reshape(own_rows, -1)
    row_keyval = (
        jnp.transpose(received[:, :, query_cols : query_cols + kv_cols], (1, 0, 2))
        .reshape(own_rows, -1)
    )
    row_keyval = lax.reduce_precision(row_keyval, 8, 7).astype(jnp.bfloat16)
    correction = jnp.sum(received[:, :, query_cols + kv_cols :], axis=0)
    row_query = lax.reduce_precision(plain_query + ADAPTER_SCALE * correction, 8, 7).astype(
        jnp.bfloat16
    )
    context = attend(row_query, row_keyval, cached_key_rows, cached_value_rows, cached_length_rows)
    heads = jnp.transpose(context.reshape(own_rows, tp, -1), (1, 0, 2))
    return project_and_scatter(heads, output_weight, tp)


def solution(mesh):
    in_specs = (
        P(("groups", "tp"), None),
        P(),
        P(None, "tp"),
        P(None, "tp"),
        P("tp", None),
        P(("groups", "tp"), None, None),
        P(("groups", "tp"), None, None),
        P(("groups", "tp"), None, None),
        P(("groups", "tp"), None, None),
        P("groups"),
        P(("groups", "tp")),
        P("groups"),
    )
    out_specs = P(("groups", "tp"), None)
    return jax.shard_map(
        on_device, mesh=mesh, in_specs=in_specs, out_specs=out_specs, check_vma=False
    )
```

```python
import functools
import math

import jax
import jax.numpy as jnp
from jax import lax
from jax.experimental import pallas as pl
from jax.experimental.pallas import tpu as pltpu
from jax.sharding import PartitionSpec as P

KV_HEADS = 8
HEAD_WIDTH = 128


EPSILON = 1e-05
ADAPTER_SCALE = 0.5
ROPE_BASE = 500000.0

VMEM_LIMIT = 24 * 1024 * 1024
CHUNKS = 4
FOLD = 8


def flip(index, bits):
    bit = 1
    while bit <= bits:
        if bits & bit:
            index = index + bit - 2 * bit * ((index // bit) % 2)
        bit *= 2
    return index


def peers(n):
    me = lax.axis_index("tp")
    outer = n // 4
    a, b, c = me // 4, (me // 2) % 2, me % 2
    core_peer = a * 4 + b * 2 + (1 - c)
    mid_peer = a * 4 + (1 - b) * 2 + c
    far = [flip(a, k) * 4 + b * 2 + c for k in range(outer)]
    return me, outer, a, b, c, core_peer, mid_peer, far


def hail(partners):
    barrier = pltpu.get_barrier_semaphore()
    for partner in partners:
        pl.semaphore_signal(
            barrier, inc=1, device_id={"tp": partner}, device_id_type=pl.DeviceIdType.MESH
        )


def meet(partners):
    pl.semaphore_wait(pltpu.get_barrier_semaphore(), len(partners))


def send(src, dst, send_sem, recv_sem, target):
    return pltpu.make_async_remote_copy(
        src_ref=src,
        dst_ref=dst,
        send_sem=send_sem,
        recv_sem=recv_sem,
        device_id={"tp": target},
        device_id_type=pl.DeviceIdType.MESH,
    )


def gather_kernel(
    n, x_ref, gain_ref, out_ref, x_fold, gain_fold, far_send, mid_send, core_send, recv
):
    me, outer, a, b, c, core_peer, mid_peer, far = peers(n)
    partners = [core_peer, mid_peer] + far[1:]
    hail(partners)
    rows, width = x_ref.shape
    fold_width = width // FOLD
    for s in range(FOLD):
        part = pl.ds(s * fold_width, fold_width)
        gain_fold[pl.ds(s, 1), :] = gain_ref[:, part]
        piece = x_ref[:, part].astype(jnp.float32)
        for r in range(rows):
            x_fold[pl.ds(r * FOLD + s, 1), :] = piece[r : r + 1, :]
    normed = []
    for r in range(rows):
        x = x_fold[pl.ds(r * FOLD, FOLD), :]
        mean = jnp.sum(x * x) / width
        normed.append(x * lax.rsqrt(mean + EPSILON) * gain_fold[...])
    out_ref[me] = jnp.concatenate(normed, axis=0).astype(jnp.bfloat16)
    meet(partners)

    def push(block, sem, target):
        copy = send(out_ref.at[block], out_ref.at[block], sem, recv.at[block], target)
        copy.start()
        return copy

    def arrived(block):
        send(out_ref.at[block], out_ref.at[block], core_send.at[0], recv.at[block], core_peer).wait_recv()

    copies = [push(me, mid_send.at[0], mid_peer)]
    copies += [push(me, far_send.at[k], far[k]) for k in range(1, outer)]
    copies.append(push(me, core_send.at[0], core_peer))
    for k in range(1, outer):
        arrived(far[k])
        copies.append(push(far[k], mid_send.at[k], mid_peer))
        copies.append(push(far[k], core_send.at[k], core_peer))
    across = [far[k] - b * 2 + (1 - b) * 2 for k in range(outer)]
    for k in range(outer):
        arrived(across[k])
        copies.append(push(across[k], core_send.at[outer + k], core_peer))
    for k in range(outer):
        arrived(far[k] - c + (1 - c))
    for k in range(outer):
        arrived(across[k] - c + (1 - c))
    for copy in copies:
        copy.wait_send()


def normalize_and_gather(tokens, gain, n):
    rows, width = tokens.shape
    fold_width = width // FOLD
    outer = n // 4
    gathered = pl.pallas_call(
        functools.partial(gather_kernel, n),
        out_shape=jax.ShapeDtypeStruct((n, rows * FOLD, fold_width), jnp.bfloat16),
        in_specs=[pl.BlockSpec(memory_space=pltpu.VMEM)] * 2,
        out_specs=pl.BlockSpec(memory_space=pltpu.VMEM),
        scratch_shapes=[
            pltpu.VMEM((rows * FOLD, fold_width), jnp.float32),
            pltpu.VMEM((FOLD, fold_width), jnp.float32),
            pltpu.SemaphoreType.DMA((outer,)),
            pltpu.SemaphoreType.DMA((outer,)),
            pltpu.SemaphoreType.DMA((2 * outer,)),
            pltpu.SemaphoreType.DMA((n,)),
        ],
        compiler_params=pltpu.CompilerParams(
            collective_id=0, has_side_effects=True, vmem_limit_bytes=VMEM_LIMIT
        ),
    )(tokens, gain.reshape(1, width))
    return gathered.reshape(n * rows, width)


def others(n):
    me = lax.axis_index("tp")
    return me, [flip(me, k) for k in range(1, n)]


def exchange_kernel(n, packed_ref, out_ref, own_sem, send_sem, recv_sem):
    me, to = others(n)
    hail(to)
    own = pltpu.make_async_copy(packed_ref.at[me], out_ref.at[me], own_sem)
    own.start()
    meet(to)
    copies = []
    for k in range(n - 1):
        copy = send(
            packed_ref.at[to[k]], out_ref.at[me], send_sem.at[k], recv_sem.at[k], to[k]
        )
        copy.start()
        copies.append(copy)
    own.wait()
    for k in range(n - 1):
        copies[k].wait_send()
        send(
            packed_ref.at[to[k]], out_ref.at[to[k]], send_sem.at[k], recv_sem.at[k], to[k]
        ).wait_recv()


def exchange(packed, n):
    return pl.pallas_call(
        functools.partial(exchange_kernel, n),
        out_shape=jax.ShapeDtypeStruct(packed.shape, packed.dtype),
        in_specs=[pl.BlockSpec(memory_space=pltpu.VMEM)],
        out_specs=pl.BlockSpec(memory_space=pltpu.VMEM),
        scratch_shapes=[
            pltpu.SemaphoreType.DMA(()),
            pltpu.SemaphoreType.DMA((n - 1,)),
            pltpu.SemaphoreType.DMA((n - 1,)),
        ],
        compiler_params=pltpu.CompilerParams(
            collective_id=2, has_side_effects=True, vmem_limit_bytes=VMEM_LIMIT
        ),
    )(packed)


def project_kernel(
    n,
    rows,
    heads_ref,
    w_ref,
    out_ref,
    h_ref,
    ctx_ref,
    p_ref,
    r1,
    r2,
    x_ref,
    r3,
    s0,
    q0,
    s1,
    q1,
    s2,
    q2,
    s3,
    q3,
):
    me, outer, a, b, c, core_peer, mid_peer, far = peers(n)
    cols = w_ref.shape[1] // CHUNKS
    quarter = outer * rows
    slot = (c * 2 + b) * outer + a
    _, to = others(n)
    hail(to)
    meet(to)
    sent = []
    for k in range(n - 1):
        copy = send(heads_ref.at[to[k]], h_ref.at[slot], s0.at[k], q0.at[slot], to[k])
        copy.start()
        sent.append(copy)
    h_ref[slot] = heads_ref[me]
    for k in range(n - 1):
        source = to[k]
        place = ((source % 2) * 2 + (source // 2) % 2) * outer + source // 4
        send(heads_ref.at[to[k]], h_ref.at[place], s0.at[k], q0.at[place], to[k]).wait_recv()
    for t in range(n):
        ctx_ref[t * rows : (t + 1) * rows, :] = h_ref[t]
    context = ctx_ref[...].astype(jnp.bfloat16)
    first, second, third = [], [], []
    for i in range(CHUNKS):
        part = jnp.dot(
            context, w_ref[:, i * cols : (i + 1) * cols], preferred_element_type=jnp.float32
        )
        p_ref[i] = part.reshape(2, 2, quarter, cols)
        copy = send(p_ref.at[i, 1 - c], r1.at[i], s1.at[i], q1.at[i], core_peer)
        copy.start()
        first.append(copy)
    for i in range(CHUNKS):
        first[i].wait()
        p_ref[i, c] = p_ref[i, c] + r1[i]
        copy = send(p_ref.at[i, c, 1 - b], r2.at[i], s2.at[i], q2.at[i], mid_peer)
        copy.start()
        second.append(copy)
    for i in range(CHUNKS):
        second[i].wait()
        both = p_ref[i, c, b] + r2[i]
        for t in range(outer):
            x_ref[i, t] = both[t * rows : (t + 1) * rows, :]
        group = []
        for k in range(1, outer):
            copy = send(
                x_ref.at[i, flip(a, k)], r3.at[i, k], s3.at[i, k], q3.at[i, k], far[k]
            )
            copy.start()
            group.append(copy)
        third.append(group)
    for i in range(CHUNKS):
        total = x_ref[i, a]
        for k in range(1, outer):
            third[i][k - 1].wait()
            total = total + r3[i, k]
        out_ref[:, i * cols : (i + 1) * cols] = total.astype(jnp.bfloat16)
    for copy in sent:
        copy.wait_send()


def project_and_scatter(heads, weight, n):
    rows, depth = heads.shape[1:]
    outer = n // 4
    width = weight.shape[1]
    cols = width // CHUNKS
    quarter = outer * rows
    return pl.pallas_call(
        functools.partial(project_kernel, n, rows),
        out_shape=jax.ShapeDtypeStruct((rows, width), jnp.bfloat16),
        in_specs=[pl.BlockSpec(memory_space=pltpu.VMEM)] * 2,
        out_specs=pl.BlockSpec(memory_space=pltpu.VMEM),
        scratch_shapes=[
            pltpu.VMEM((n, rows, depth), jnp.float32),
            pltpu.VMEM((n * rows, depth), jnp.float32),
            pltpu.VMEM((CHUNKS, 2, 2, quarter, cols), jnp.float32),
            pltpu.VMEM((CHUNKS, 2, quarter, cols), jnp.float32),
            pltpu.VMEM((CHUNKS, quarter, cols), jnp.float32),
            pltpu.VMEM((CHUNKS, outer, rows, cols), jnp.float32),
            pltpu.VMEM((CHUNKS, outer, rows, cols), jnp.float32),
            pltpu.SemaphoreType.DMA((n,)),
            pltpu.SemaphoreType.DMA((n,)),
            pltpu.SemaphoreType.DMA((CHUNKS,)),
            pltpu.SemaphoreType.DMA((CHUNKS,)),
            pltpu.SemaphoreType.DMA((CHUNKS,)),
            pltpu.SemaphoreType.DMA((CHUNKS,)),
            pltpu.SemaphoreType.DMA((CHUNKS, outer)),
            pltpu.SemaphoreType.DMA((CHUNKS, outer)),
        ],
        compiler_params=pltpu.CompilerParams(
            collective_id=1, has_side_effects=True, vmem_limit_bytes=VMEM_LIMIT
        ),
    )(heads, weight)


def rotate(values_in, places):
    half_size = HEAD_WIDTH // 2
    freqs = ROPE_BASE ** (-jnp.arange(half_size, dtype=jnp.float32) / half_size)
    angles = places.astype(jnp.float32)[:, None, None] * freqs[None, None, :]
    cosine = jnp.cos(angles)
    sine = jnp.sin(angles)
    first_half = values_in[..., :half_size]
    second_half = values_in[..., half_size:]
    return jnp.concatenate(
        [first_half * cosine - second_half * sine, second_half * cosine + first_half * sine],
        axis=-1,
    )


def attend(query_vector, keyval, cached_key_rows, cached_value_rows, lengths_here):
    row_count = query_vector.shape[0]
    head_count = query_vector.shape[1] // HEAD_WIDTH
    group_size = head_count // KV_HEADS
    kv_width = KV_HEADS * HEAD_WIDTH
    queries = rotate(
        query_vector.astype(jnp.float32).reshape(row_count, head_count, HEAD_WIDTH), lengths_here
    ).astype(jnp.bfloat16)
    new_keys = rotate(
        keyval[:, :kv_width].astype(jnp.float32).reshape(row_count, KV_HEADS, HEAD_WIDTH),
        lengths_here,
    ).astype(jnp.bfloat16)
    new_values = keyval[:, kv_width:].reshape(row_count, KV_HEADS, HEAD_WIDTH)
    grouped = queries.reshape(row_count, KV_HEADS, group_size, HEAD_WIDTH)
    old_keys = cached_key_rows.reshape(row_count, -1, KV_HEADS, HEAD_WIDTH)
    old_values = cached_value_rows.reshape(row_count, -1, KV_HEADS, HEAD_WIDTH)
    factor = 1.0 / math.sqrt(HEAD_WIDTH)
    scores = (
        jnp.einsum("rgqd,rcgd->rgqc", grouped, old_keys, preferred_element_type=jnp.float32)
        * factor
    )
    own_score = (
        jnp.einsum("rgqd,rgd->rgq", grouped, new_keys, preferred_element_type=jnp.float32) * factor
    )
    valid = jnp.arange(old_keys.shape[1], dtype=jnp.int32)[None, :] < lengths_here[:, None]
    scores = jnp.where(valid[:, None, None, :], scores, -jnp.inf)
    highest = jnp.maximum(jnp.max(scores, axis=-1), own_score)
    expos = jnp.exp(scores - highest[..., None])
    own_expo = jnp.exp(own_score - highest)
    total = jnp.sum(expos, axis=-1) + own_expo
    weights = (expos / total[..., None]).astype(jnp.bfloat16)
    own_weight = (own_expo / total).astype(jnp.bfloat16)
    context = jnp.einsum("rgqc,rcgd->rgqd", weights, old_values, preferred_element_type=jnp.float32)
    context = (
        context
        + own_weight.astype(jnp.float32)[..., None] * new_values.astype(jnp.float32)[:, :, None, :]
    )
    return context.reshape(row_count, head_count * HEAD_WIDTH)


def on_device(
    tokens,
    norm_gain_vector,
    query_weight,
    key_value_weight,
    output_weight,
    adapter_down_factor,
    adapter_up_factor,
    cached_key_rows,
    cached_value_rows,
    row_adapter_index,
    cached_length_rows,
    adapter_slot_index,
):
    position = lax.axis_index("tp")
    tp = lax.axis_size("tp")
    adapter_count = adapter_slot_index.shape[0]
    resident_count = adapter_down_factor.shape[0]
    rank_width = adapter_down_factor.shape[2]
    hidden_width = adapter_down_factor.shape[1]
    table = row_adapter_index[:, None] == jnp.arange(adapter_count, dtype=jnp.int32)[None, :]
    slot = jnp.sum(jnp.where(table, adapter_slot_index[None, :], 0), axis=1)
    local_slots = position * resident_count + jnp.arange(resident_count, dtype=jnp.int32)
    owned = slot[:, None] == local_slots[None, :]
    down_factor_rows = jnp.transpose(adapter_down_factor, (1, 0, 2)).reshape(
        hidden_width, resident_count * rank_width
    )
    query_cols = query_weight.shape[1]
    kv_cols = key_value_weight.shape[1]
    piece = normalize_and_gather(tokens, norm_gain_vector, tp)
    piece_rows = piece.shape[0]
    query_part = jnp.dot(piece, query_weight, preferred_element_type=jnp.float32)
    kv_part = jnp.dot(piece, key_value_weight, preferred_element_type=jnp.float32)
    low_part = jnp.dot(piece, down_factor_rows, preferred_element_type=jnp.float32).reshape(
        piece_rows, resident_count, rank_width
    )
    low = low_part.astype(jnp.bfloat16)
    masked_low = jnp.where(owned[:, :, None], low, jnp.zeros((), jnp.bfloat16)).reshape(
        piece_rows, resident_count * rank_width
    )
    up_factor_rows = adapter_up_factor.reshape(
        resident_count * rank_width, adapter_up_factor.shape[2]
    )
    terms = jnp.dot(masked_low, up_factor_rows, preferred_element_type=jnp.float32)
    packed = jnp.concatenate([query_part, kv_part, terms], axis=1)
    packed = packed.reshape(tp, piece_rows // tp, packed.shape[1])
    received = exchange(packed, tp)
    own_rows = piece_rows // tp
    plain_query = jnp.transpose(received[:, :, :query_cols], (1, 0, 2)).reshape(own_rows, -1)
    row_keyval = (
        jnp.transpose(received[:, :, query_cols : query_cols + kv_cols], (1, 0, 2))
        .reshape(own_rows, -1)
    )
    row_keyval = lax.reduce_precision(row_keyval, 8, 7).astype(jnp.bfloat16)
    correction = jnp.sum(received[:, :, query_cols + kv_cols :], axis=0)
    row_query = lax.reduce_precision(plain_query + ADAPTER_SCALE * correction, 8, 7).astype(
        jnp.bfloat16
    )
    context = attend(row_query, row_keyval, cached_key_rows, cached_value_rows, cached_length_rows)
    heads = jnp.transpose(context.reshape(own_rows, tp, -1), (1, 0, 2))
    return project_and_scatter(heads, output_weight, tp)


def solution(mesh):
    in_specs = (
        P(("groups", "tp"), None),
        P(),
        P(None, "tp"),
        P(None, "tp"),
        P("tp", None),
        P(("groups", "tp"), None, None),
        P(("groups", "tp"), None, None),
        P(("groups", "tp"), None, None),
        P(("groups", "tp"), None, None),
        P("groups"),
        P(("groups", "tp")),
        P("groups"),
    )
    out_specs = P(("groups", "tp"), None)
    return jax.shard_map(
        on_device, mesh=mesh, in_specs=in_specs, out_specs=out_specs, check_vma=False
    )
```

```python
import functools
import math

import jax
import jax.numpy as jnp
from jax import lax
from jax.experimental import pallas as pl
from jax.experimental.pallas import tpu as pltpu
from jax.sharding import PartitionSpec as P

KV_HEADS = 8
HEAD_WIDTH = 128


EPSILON = 1e-05
ADAPTER_SCALE = 0.5
ROPE_BASE = 500000.0

VMEM_LIMIT = 24 * 1024 * 1024
CHUNKS = 8
FOLD = 8


def flip(index, bits):
    bit = 1
    while bit <= bits:
        if bits & bit:
            index = index + bit - 2 * bit * ((index // bit) % 2)
        bit *= 2
    return index


def peers(n):
    me = lax.axis_index("tp")
    outer = n // 4
    a, b, c = me // 4, (me // 2) % 2, me % 2
    core_peer = a * 4 + b * 2 + (1 - c)
    mid_peer = a * 4 + (1 - b) * 2 + c
    far = [flip(a, k) * 4 + b * 2 + c for k in range(outer)]
    return me, outer, a, b, c, core_peer, mid_peer, far


def hail(partners):
    barrier = pltpu.get_barrier_semaphore()
    for partner in partners:
        pl.semaphore_signal(
            barrier, inc=1, device_id={"tp": partner}, device_id_type=pl.DeviceIdType.MESH
        )


def meet(partners):
    pl.semaphore_wait(pltpu.get_barrier_semaphore(), len(partners))


def send(src, dst, send_sem, recv_sem, target):
    return pltpu.make_async_remote_copy(
        src_ref=src,
        dst_ref=dst,
        send_sem=send_sem,
        recv_sem=recv_sem,
        device_id={"tp": target},
        device_id_type=pl.DeviceIdType.MESH,
    )


def gather_kernel(
    n, x_ref, gain_hbm, out_ref, gain_ref, x_fold, gain_fold, load, far_send, mid_send, core_send, recv
):
    me, outer, a, b, c, core_peer, mid_peer, far = peers(n)
    partners = [core_peer, mid_peer] + far[1:]
    fetch = pltpu.make_async_copy(gain_hbm, gain_ref, load)
    fetch.start()
    hail(partners)
    rows, width = x_ref.shape
    fold_width = width // FOLD
    for s in range(FOLD):
        part = pl.ds(s * fold_width, fold_width)
        piece = x_ref[:, part].astype(jnp.float32)
        for r in range(rows):
            x_fold[pl.ds(r * FOLD + s, 1), :] = piece[r : r + 1, :]
    fetch.wait()
    for s in range(FOLD):
        gain_fold[pl.ds(s, 1), :] = gain_ref[:, pl.ds(s * fold_width, fold_width)]
    normed = []
    for r in range(rows):
        x = x_fold[pl.ds(r * FOLD, FOLD), :]
        mean = jnp.sum(x * x) / width
        normed.append(x * lax.rsqrt(mean + EPSILON) * gain_fold[...])
    out_ref[me] = jnp.concatenate(normed, axis=0).astype(jnp.bfloat16)
    meet(partners)

    def push(block, sem, target):
        copy = send(out_ref.at[block], out_ref.at[block], sem, recv.at[block], target)
        copy.start()
        return copy

    def arrived(block):
        send(out_ref.at[block], out_ref.at[block], core_send.at[0], recv.at[block], core_peer).wait_recv()

    copies = [push(me, mid_send.at[0], mid_peer)]
    copies += [push(me, far_send.at[k], far[k]) for k in range(1, outer)]
    copies.append(push(me, core_send.at[0], core_peer))
    for k in range(1, outer):
        arrived(far[k])
        copies.append(push(far[k], mid_send.at[k], mid_peer))
        copies.append(push(far[k], core_send.at[k], core_peer))
    across = [far[k] - b * 2 + (1 - b) * 2 for k in range(outer)]
    for k in range(outer):
        arrived(across[k])
        copies.append(push(across[k], core_send.at[outer + k], core_peer))
    for k in range(outer):
        arrived(far[k] - c + (1 - c))
    for k in range(outer):
        arrived(across[k] - c + (1 - c))
    for copy in copies:
        copy.wait_send()


def normalize_and_gather(tokens, gain, n):
    rows, width = tokens.shape
    fold_width = width // FOLD
    outer = n // 4
    gathered = pl.pallas_call(
        functools.partial(gather_kernel, n),
        out_shape=jax.ShapeDtypeStruct((n, rows * FOLD, fold_width), jnp.bfloat16),
        in_specs=[pl.BlockSpec(memory_space=pltpu.VMEM), pl.BlockSpec(memory_space=pl.ANY)],
        out_specs=pl.BlockSpec(memory_space=pltpu.VMEM),
        scratch_shapes=[
            pltpu.VMEM((1, width), jnp.float32),
            pltpu.VMEM((rows * FOLD, fold_width), jnp.float32),
            pltpu.VMEM((FOLD, fold_width), jnp.float32),
            pltpu.SemaphoreType.DMA(()),
            pltpu.SemaphoreType.DMA((outer,)),
            pltpu.SemaphoreType.DMA((outer,)),
            pltpu.SemaphoreType.DMA((2 * outer,)),
            pltpu.SemaphoreType.DMA((n,)),
        ],
        compiler_params=pltpu.CompilerParams(
            collective_id=0, has_side_effects=True, vmem_limit_bytes=VMEM_LIMIT
        ),
    )(tokens, gain.reshape(1, width))
    return gathered.reshape(n * rows, width)


def others(n):
    me = lax.axis_index("tp")
    return me, [flip(me, k) for k in range(1, n)]


def exchange_kernel(n, packed_ref, out_ref, own_sem, send_sem, recv_sem):
    me, to = others(n)
    hail(to)
    own = pltpu.make_async_copy(packed_ref.at[me], out_ref.at[me], own_sem)
    own.start()
    meet(to)
    copies = []
    for k in range(n - 1):
        copy = send(
            packed_ref.at[to[k]], out_ref.at[me], send_sem.at[k], recv_sem.at[k], to[k]
        )
        copy.start()
        copies.append(copy)
    own.wait()
    for k in range(n - 1):
        copies[k].wait_send()
        send(
            packed_ref.at[to[k]], out_ref.at[to[k]], send_sem.at[k], recv_sem.at[k], to[k]
        ).wait_recv()


def exchange(packed, n):
    return pl.pallas_call(
        functools.partial(exchange_kernel, n),
        out_shape=jax.ShapeDtypeStruct(packed.shape, packed.dtype),
        in_specs=[pl.BlockSpec(memory_space=pltpu.VMEM)],
        out_specs=pl.BlockSpec(memory_space=pltpu.VMEM),
        scratch_shapes=[
            pltpu.SemaphoreType.DMA(()),
            pltpu.SemaphoreType.DMA((n - 1,)),
            pltpu.SemaphoreType.DMA((n - 1,)),
        ],
        compiler_params=pltpu.CompilerParams(
            collective_id=2, has_side_effects=True, vmem_limit_bytes=VMEM_LIMIT
        ),
    )(packed)


def project_kernel(
    n,
    rows,
    heads_ref,
    w_ref,
    out_ref,
    h_ref,
    ctx_ref,
    p_ref,
    r1,
    r2,
    x_ref,
    r3,
    s0,
    q0,
    s1,
    q1,
    s2,
    q2,
    s3,
    q3,
):
    me, outer, a, b, c, core_peer, mid_peer, far = peers(n)
    cols = w_ref.shape[1] // CHUNKS
    quarter = outer * rows
    slot = (c * 2 + b) * outer + a
    _, to = others(n)
    hail(to)
    meet(to)
    sent = []
    for k in range(n - 1):
        copy = send(heads_ref.at[to[k]], h_ref.at[slot], s0.at[k], q0.at[slot], to[k])
        copy.start()
        sent.append(copy)
    h_ref[slot] = heads_ref[me]
    for k in range(n - 1):
        source = to[k]
        place = ((source % 2) * 2 + (source // 2) % 2) * outer + source // 4
        send(heads_ref.at[to[k]], h_ref.at[place], s0.at[k], q0.at[place], to[k]).wait_recv()
    for t in range(n):
        ctx_ref[t * rows : (t + 1) * rows, :] = h_ref[t]
    context = ctx_ref[...].astype(jnp.bfloat16)
    first, second, third = [], [], []
    for i in range(CHUNKS):
        part = jnp.dot(
            context, w_ref[:, i * cols : (i + 1) * cols], preferred_element_type=jnp.float32
        )
        p_ref[i] = part.reshape(2, 2, quarter, cols)
        copy = send(p_ref.at[i, 1 - c], r1.at[i], s1.at[i], q1.at[i], core_peer)
        copy.start()
        first.append(copy)
    for i in range(CHUNKS):
        first[i].wait()
        p_ref[i, c] = p_ref[i, c] + r1[i]
        copy = send(p_ref.at[i, c, 1 - b], r2.at[i], s2.at[i], q2.at[i], mid_peer)
        copy.start()
        second.append(copy)
    for i in range(CHUNKS):
        second[i].wait()
        both = p_ref[i, c, b] + r2[i]
        for t in range(outer):
            x_ref[i, t] = both[t * rows : (t + 1) * rows, :]
        group = []
        for k in range(1, outer):
            copy = send(
                x_ref.at[i, flip(a, k)], r3.at[i, k], s3.at[i, k], q3.at[i, k], far[k]
            )
            copy.start()
            group.append(copy)
        third.append(group)
    for i in range(CHUNKS):
        total = x_ref[i, a]
        for k in range(1, outer):
            third[i][k - 1].wait()
            total = total + r3[i, k]
        out_ref[:, i * cols : (i + 1) * cols] = total.astype(jnp.bfloat16)
    for copy in sent:
        copy.wait_send()


def project_and_scatter(heads, weight, n):
    rows, depth = heads.shape[1:]
    outer = n // 4
    width = weight.shape[1]
    cols = width // CHUNKS
    quarter = outer * rows
    return pl.pallas_call(
        functools.partial(project_kernel, n, rows),
        out_shape=jax.ShapeDtypeStruct((rows, width), jnp.bfloat16),
        in_specs=[pl.BlockSpec(memory_space=pltpu.VMEM)] * 2,
        out_specs=pl.BlockSpec(memory_space=pltpu.VMEM),
        scratch_shapes=[
            pltpu.VMEM((n, rows, depth), jnp.float32),
            pltpu.VMEM((n * rows, depth), jnp.float32),
            pltpu.VMEM((CHUNKS, 2, 2, quarter, cols), jnp.float32),
            pltpu.VMEM((CHUNKS, 2, quarter, cols), jnp.float32),
            pltpu.VMEM((CHUNKS, quarter, cols), jnp.float32),
            pltpu.VMEM((CHUNKS, outer, rows, cols), jnp.float32),
            pltpu.VMEM((CHUNKS, outer, rows, cols), jnp.float32),
            pltpu.SemaphoreType.DMA((n,)),
            pltpu.SemaphoreType.DMA((n,)),
            pltpu.SemaphoreType.DMA((CHUNKS,)),
            pltpu.SemaphoreType.DMA((CHUNKS,)),
            pltpu.SemaphoreType.DMA((CHUNKS,)),
            pltpu.SemaphoreType.DMA((CHUNKS,)),
            pltpu.SemaphoreType.DMA((CHUNKS, outer)),
            pltpu.SemaphoreType.DMA((CHUNKS, outer)),
        ],
        compiler_params=pltpu.CompilerParams(
            collective_id=1, has_side_effects=True, vmem_limit_bytes=VMEM_LIMIT
        ),
    )(heads, weight)


def rotate(values_in, places):
    half_size = HEAD_WIDTH // 2
    freqs = ROPE_BASE ** (-jnp.arange(half_size, dtype=jnp.float32) / half_size)
    angles = places.astype(jnp.float32)[:, None, None] * freqs[None, None, :]
    cosine = jnp.cos(angles)
    sine = jnp.sin(angles)
    first_half = values_in[..., :half_size]
    second_half = values_in[..., half_size:]
    return jnp.concatenate(
        [first_half * cosine - second_half * sine, second_half * cosine + first_half * sine],
        axis=-1,
    )


def attend(query_vector, keyval, cached_key_rows, cached_value_rows, lengths_here):
    row_count = query_vector.shape[0]
    head_count = query_vector.shape[1] // HEAD_WIDTH
    group_size = head_count // KV_HEADS
    kv_width = KV_HEADS * HEAD_WIDTH
    queries = rotate(
        query_vector.astype(jnp.float32).reshape(row_count, head_count, HEAD_WIDTH), lengths_here
    ).astype(jnp.bfloat16)
    new_keys = rotate(
        keyval[:, :kv_width].astype(jnp.float32).reshape(row_count, KV_HEADS, HEAD_WIDTH),
        lengths_here,
    ).astype(jnp.bfloat16)
    new_values = keyval[:, kv_width:].reshape(row_count, KV_HEADS, HEAD_WIDTH)
    grouped = queries.reshape(row_count, KV_HEADS, group_size, HEAD_WIDTH)
    old_keys = cached_key_rows.reshape(row_count, -1, KV_HEADS, HEAD_WIDTH)
    old_values = cached_value_rows.reshape(row_count, -1, KV_HEADS, HEAD_WIDTH)
    factor = 1.0 / math.sqrt(HEAD_WIDTH)
    scores = (
        jnp.einsum("rgqd,rcgd->rgqc", grouped, old_keys, preferred_element_type=jnp.float32)
        * factor
    )
    own_score = (
        jnp.einsum("rgqd,rgd->rgq", grouped, new_keys, preferred_element_type=jnp.float32) * factor
    )
    valid = jnp.arange(old_keys.shape[1], dtype=jnp.int32)[None, :] < lengths_here[:, None]
    scores = jnp.where(valid[:, None, None, :], scores, -jnp.inf)
    highest = jnp.maximum(jnp.max(scores, axis=-1), own_score)
    expos = jnp.exp(scores - highest[..., None])
    own_expo = jnp.exp(own_score - highest)
    total = jnp.sum(expos, axis=-1) + own_expo
    weights = (expos / total[..., None]).astype(jnp.bfloat16)
    own_weight = (own_expo / total).astype(jnp.bfloat16)
    context = jnp.einsum("rgqc,rcgd->rgqd", weights, old_values, preferred_element_type=jnp.float32)
    context = (
        context
        + own_weight.astype(jnp.float32)[..., None] * new_values.astype(jnp.float32)[:, :, None, :]
    )
    return context.reshape(row_count, head_count * HEAD_WIDTH)


def on_device(
    tokens,
    norm_gain_vector,
    query_weight,
    key_value_weight,
    output_weight,
    adapter_down_factor,
    adapter_up_factor,
    cached_key_rows,
    cached_value_rows,
    row_adapter_index,
    cached_length_rows,
    adapter_slot_index,
):
    position = lax.axis_index("tp")
    tp = lax.axis_size("tp")
    adapter_count = adapter_slot_index.shape[0]
    resident_count = adapter_down_factor.shape[0]
    rank_width = adapter_down_factor.shape[2]
    hidden_width = adapter_down_factor.shape[1]
    table = row_adapter_index[:, None] == jnp.arange(adapter_count, dtype=jnp.int32)[None, :]
    slot = jnp.sum(jnp.where(table, adapter_slot_index[None, :], 0), axis=1)
    local_slots = position * resident_count + jnp.arange(resident_count, dtype=jnp.int32)
    owned = slot[:, None] == local_slots[None, :]
    down_factor_rows = jnp.transpose(adapter_down_factor, (1, 0, 2)).reshape(
        hidden_width, resident_count * rank_width
    )
    query_cols = query_weight.shape[1]
    kv_cols = key_value_weight.shape[1]
    piece = normalize_and_gather(tokens, norm_gain_vector, tp)
    piece_rows = piece.shape[0]
    query_part = jnp.dot(piece, query_weight, preferred_element_type=jnp.float32)
    kv_part = jnp.dot(piece, key_value_weight, preferred_element_type=jnp.float32)
    low_part = jnp.dot(piece, down_factor_rows, preferred_element_type=jnp.float32).reshape(
        piece_rows, resident_count, rank_width
    )
    low = low_part.astype(jnp.bfloat16)
    masked_low = jnp.where(owned[:, :, None], low, jnp.zeros((), jnp.bfloat16)).reshape(
        piece_rows, resident_count * rank_width
    )
    up_factor_rows = adapter_up_factor.reshape(
        resident_count * rank_width, adapter_up_factor.shape[2]
    )
    terms = jnp.dot(masked_low, up_factor_rows, preferred_element_type=jnp.float32)
    packed = jnp.concatenate([query_part, kv_part, terms], axis=1)
    packed = packed.reshape(tp, piece_rows // tp, packed.shape[1])
    received = exchange(packed, tp)
    own_rows = piece_rows // tp
    plain_query = jnp.transpose(received[:, :, :query_cols], (1, 0, 2)).reshape(own_rows, -1)
    row_keyval = (
        jnp.transpose(received[:, :, query_cols : query_cols + kv_cols], (1, 0, 2))
        .reshape(own_rows, -1)
    )
    row_keyval = lax.reduce_precision(row_keyval, 8, 7).astype(jnp.bfloat16)
    correction = jnp.sum(received[:, :, query_cols + kv_cols :], axis=0)
    row_query = lax.reduce_precision(plain_query + ADAPTER_SCALE * correction, 8, 7).astype(
        jnp.bfloat16
    )
    context = attend(row_query, row_keyval, cached_key_rows, cached_value_rows, cached_length_rows)
    heads = jnp.transpose(context.reshape(own_rows, tp, -1), (1, 0, 2))
    return project_and_scatter(heads, output_weight, tp)


def solution(mesh):
    in_specs = (
        P(("groups", "tp"), None),
        P(),
        P(None, "tp"),
        P(None, "tp"),
        P("tp", None),
        P(("groups", "tp"), None, None),
        P(("groups", "tp"), None, None),
        P(("groups", "tp"), None, None),
        P(("groups", "tp"), None, None),
        P("groups"),
        P(("groups", "tp")),
        P("groups"),
    )
    out_specs = P(("groups", "tp"), None)
    return jax.shard_map(
        on_device, mesh=mesh, in_specs=in_specs, out_specs=out_specs, check_vma=False
    )
```

```python
import functools
import math

import jax
import jax.numpy as jnp
from jax import lax
from jax.experimental import pallas as pl
from jax.experimental.pallas import tpu as pltpu
from jax.sharding import PartitionSpec as P

KV_HEADS = 8
HEAD_WIDTH = 128


EPSILON = 1e-05
ADAPTER_SCALE = 0.5
ROPE_BASE = 500000.0

VMEM_LIMIT = 24 * 1024 * 1024
CHUNKS = 8
FOLD = 8


def flip(index, bits):
    bit = 1
    while bit <= bits:
        if bits & bit:
            index = index + bit - 2 * bit * ((index // bit) % 2)
        bit *= 2
    return index


def peers(n):
    me = lax.axis_index("tp")
    outer = n // 4
    a, b, c = me // 4, (me // 2) % 2, me % 2
    core_peer = a * 4 + b * 2 + (1 - c)
    mid_peer = a * 4 + (1 - b) * 2 + c
    far = [flip(a, k) * 4 + b * 2 + c for k in range(outer)]
    return me, outer, a, b, c, core_peer, mid_peer, far


def hail(partners):
    barrier = pltpu.get_barrier_semaphore()
    for partner in partners:
        pl.semaphore_signal(
            barrier, inc=1, device_id={"tp": partner}, device_id_type=pl.DeviceIdType.MESH
        )


def meet(partners):
    pl.semaphore_wait(pltpu.get_barrier_semaphore(), len(partners))


def send(src, dst, send_sem, recv_sem, target):
    return pltpu.make_async_remote_copy(
        src_ref=src,
        dst_ref=dst,
        send_sem=send_sem,
        recv_sem=recv_sem,
        device_id={"tp": target},
        device_id_type=pl.DeviceIdType.MESH,
    )


def gather_kernel(
    n, x_ref, gain_hbm, out_ref, gain_ref, x_fold, gain_fold, load, far_send, mid_send, core_send, recv
):
    me, outer, a, b, c, core_peer, mid_peer, far = peers(n)
    partners = [core_peer, mid_peer] + far[1:]
    fetch = pltpu.make_async_copy(gain_hbm, gain_ref, load)
    fetch.start()
    hail(partners)
    rows, width = x_ref.shape
    fold_width = width // FOLD
    for s in range(FOLD):
        part = pl.ds(s * fold_width, fold_width)
        piece = x_ref[:, part].astype(jnp.float32)
        for r in range(rows):
            x_fold[pl.ds(r * FOLD + s, 1), :] = piece[r : r + 1, :]
    fetch.wait()
    for s in range(FOLD):
        gain_fold[pl.ds(s, 1), :] = gain_ref[:, pl.ds(s * fold_width, fold_width)]
    normed = []
    for r in range(rows):
        x = x_fold[pl.ds(r * FOLD, FOLD), :]
        mean = jnp.sum(x * x) / width
        normed.append(x * lax.rsqrt(mean + EPSILON) * gain_fold[...])
    out_ref[me] = jnp.concatenate(normed, axis=0).astype(jnp.bfloat16)
    meet(partners)

    def push(block, sem, target):
        copy = send(out_ref.at[block], out_ref.at[block], sem, recv.at[block], target)
        copy.start()
        return copy

    def arrived(block):
        send(out_ref.at[block], out_ref.at[block], core_send.at[0], recv.at[block], core_peer).wait_recv()

    copies = [push(me, mid_send.at[0], mid_peer)]
    copies += [push(me, far_send.at[k], far[k]) for k in range(1, outer)]
    copies.append(push(me, core_send.at[0], core_peer))
    for k in range(1, outer):
        arrived(far[k])
        copies.append(push(far[k], mid_send.at[k], mid_peer))
        copies.append(push(far[k], core_send.at[k], core_peer))
    across = [far[k] - b * 2 + (1 - b) * 2 for k in range(outer)]
    for k in range(outer):
        arrived(across[k])
        copies.append(push(across[k], core_send.at[outer + k], core_peer))
    for k in range(outer):
        arrived(far[k] - c + (1 - c))
    for k in range(outer):
        arrived(across[k] - c + (1 - c))
    for copy in copies:
        copy.wait_send()


def normalize_and_gather(tokens, gain, n):
    rows, width = tokens.shape
    fold_width = width // FOLD
    outer = n // 4
    gathered = pl.pallas_call(
        functools.partial(gather_kernel, n),
        out_shape=jax.ShapeDtypeStruct((n, rows * FOLD, fold_width), jnp.bfloat16),
        in_specs=[pl.BlockSpec(memory_space=pltpu.VMEM), pl.BlockSpec(memory_space=pltpu.HBM)],
        out_specs=pl.BlockSpec(memory_space=pltpu.VMEM),
        scratch_shapes=[
            pltpu.VMEM((1, width), jnp.float32),
            pltpu.VMEM((rows * FOLD, fold_width), jnp.float32),
            pltpu.VMEM((FOLD, fold_width), jnp.float32),
            pltpu.SemaphoreType.DMA(()),
            pltpu.SemaphoreType.DMA((outer,)),
            pltpu.SemaphoreType.DMA((outer,)),
            pltpu.SemaphoreType.DMA((2 * outer,)),
            pltpu.SemaphoreType.DMA((n,)),
        ],
        compiler_params=pltpu.CompilerParams(
            collective_id=0, has_side_effects=True, vmem_limit_bytes=VMEM_LIMIT
        ),
    )(tokens, gain.reshape(1, width))
    return gathered.reshape(n * rows, width)


def others(n):
    me = lax.axis_index("tp")
    return me, [flip(me, k) for k in range(1, n)]


def exchange_kernel(n, packed_ref, out_ref, own_sem, send_sem, recv_sem):
    me, to = others(n)
    hail(to)
    own = pltpu.make_async_copy(packed_ref.at[me], out_ref.at[me], own_sem)
    own.start()
    meet(to)
    copies = []
    for k in range(n - 1):
        copy = send(
            packed_ref.at[to[k]], out_ref.at[me], send_sem.at[k], recv_sem.at[k], to[k]
        )
        copy.start()
        copies.append(copy)
    own.wait()
    for k in range(n - 1):
        copies[k].wait_send()
        send(
            packed_ref.at[to[k]], out_ref.at[to[k]], send_sem.at[k], recv_sem.at[k], to[k]
        ).wait_recv()


def exchange(packed, n):
    return pl.pallas_call(
        functools.partial(exchange_kernel, n),
        out_shape=jax.ShapeDtypeStruct(packed.shape, packed.dtype),
        in_specs=[pl.BlockSpec(memory_space=pltpu.VMEM)],
        out_specs=pl.BlockSpec(memory_space=pltpu.VMEM),
        scratch_shapes=[
            pltpu.SemaphoreType.DMA(()),
            pltpu.SemaphoreType.DMA((n - 1,)),
            pltpu.SemaphoreType.DMA((n - 1,)),
        ],
        compiler_params=pltpu.CompilerParams(
            collective_id=2, has_side_effects=True, vmem_limit_bytes=VMEM_LIMIT
        ),
    )(packed)


def project_kernel(
    n,
    rows,
    heads_ref,
    w_ref,
    out_ref,
    h_ref,
    ctx_ref,
    p_ref,
    r1,
    r2,
    x_ref,
    r3,
    s0,
    q0,
    s1,
    q1,
    s2,
    q2,
    s3,
    q3,
):
    me, outer, a, b, c, core_peer, mid_peer, far = peers(n)
    cols = w_ref.shape[1] // CHUNKS
    quarter = outer * rows
    slot = (c * 2 + b) * outer + a
    _, to = others(n)
    hail(to)
    meet(to)
    sent = []
    for k in range(n - 1):
        copy = send(heads_ref.at[to[k]], h_ref.at[slot], s0.at[k], q0.at[slot], to[k])
        copy.start()
        sent.append(copy)
    h_ref[slot] = heads_ref[me]
    for k in range(n - 1):
        source = to[k]
        place = ((source % 2) * 2 + (source // 2) % 2) * outer + source // 4
        send(heads_ref.at[to[k]], h_ref.at[place], s0.at[k], q0.at[place], to[k]).wait_recv()
    for t in range(n):
        ctx_ref[t * rows : (t + 1) * rows, :] = h_ref[t]
    context = ctx_ref[...].astype(jnp.bfloat16)
    first, second, third = [], [], []
    for i in range(CHUNKS):
        part = jnp.dot(
            context, w_ref[:, i * cols : (i + 1) * cols], preferred_element_type=jnp.float32
        )
        p_ref[i] = part.reshape(2, 2, quarter, cols)
        copy = send(p_ref.at[i, 1 - c], r1.at[i], s1.at[i], q1.at[i], core_peer)
        copy.start()
        first.append(copy)
    for i in range(CHUNKS):
        first[i].wait()
        p_ref[i, c] = p_ref[i, c] + r1[i]
        copy = send(p_ref.at[i, c, 1 - b], r2.at[i], s2.at[i], q2.at[i], mid_peer)
        copy.start()
        second.append(copy)
    for i in range(CHUNKS):
        second[i].wait()
        both = p_ref[i, c, b] + r2[i]
        for t in range(outer):
            x_ref[i, t] = both[t * rows : (t + 1) * rows, :]
        group = []
        for k in range(1, outer):
            copy = send(
                x_ref.at[i, flip(a, k)], r3.at[i, k], s3.at[i, k], q3.at[i, k], far[k]
            )
            copy.start()
            group.append(copy)
        third.append(group)
    for i in range(CHUNKS):
        total = x_ref[i, a]
        for k in range(1, outer):
            third[i][k - 1].wait()
            total = total + r3[i, k]
        out_ref[:, i * cols : (i + 1) * cols] = total.astype(jnp.bfloat16)
    for copy in sent:
        copy.wait_send()


def project_and_scatter(heads, weight, n):
    rows, depth = heads.shape[1:]
    outer = n // 4
    width = weight.shape[1]
    cols = width // CHUNKS
    quarter = outer * rows
    return pl.pallas_call(
        functools.partial(project_kernel, n, rows),
        out_shape=jax.ShapeDtypeStruct((rows, width), jnp.bfloat16),
        in_specs=[pl.BlockSpec(memory_space=pltpu.VMEM)] * 2,
        out_specs=pl.BlockSpec(memory_space=pltpu.VMEM),
        scratch_shapes=[
            pltpu.VMEM((n, rows, depth), jnp.float32),
            pltpu.VMEM((n * rows, depth), jnp.float32),
            pltpu.VMEM((CHUNKS, 2, 2, quarter, cols), jnp.float32),
            pltpu.VMEM((CHUNKS, 2, quarter, cols), jnp.float32),
            pltpu.VMEM((CHUNKS, quarter, cols), jnp.float32),
            pltpu.VMEM((CHUNKS, outer, rows, cols), jnp.float32),
            pltpu.VMEM((CHUNKS, outer, rows, cols), jnp.float32),
            pltpu.SemaphoreType.DMA((n,)),
            pltpu.SemaphoreType.DMA((n,)),
            pltpu.SemaphoreType.DMA((CHUNKS,)),
            pltpu.SemaphoreType.DMA((CHUNKS,)),
            pltpu.SemaphoreType.DMA((CHUNKS,)),
            pltpu.SemaphoreType.DMA((CHUNKS,)),
            pltpu.SemaphoreType.DMA((CHUNKS, outer)),
            pltpu.SemaphoreType.DMA((CHUNKS, outer)),
        ],
        compiler_params=pltpu.CompilerParams(
            collective_id=1, has_side_effects=True, vmem_limit_bytes=VMEM_LIMIT
        ),
    )(heads, weight)


def rotate(values_in, places):
    half_size = HEAD_WIDTH // 2
    freqs = ROPE_BASE ** (-jnp.arange(half_size, dtype=jnp.float32) / half_size)
    angles = places.astype(jnp.float32)[:, None, None] * freqs[None, None, :]
    cosine = jnp.cos(angles)
    sine = jnp.sin(angles)
    first_half = values_in[..., :half_size]
    second_half = values_in[..., half_size:]
    return jnp.concatenate(
        [first_half * cosine - second_half * sine, second_half * cosine + first_half * sine],
        axis=-1,
    )


def attend(query_vector, keyval, cached_key_rows, cached_value_rows, lengths_here):
    row_count = query_vector.shape[0]
    head_count = query_vector.shape[1] // HEAD_WIDTH
    group_size = head_count // KV_HEADS
    kv_width = KV_HEADS * HEAD_WIDTH
    queries = rotate(
        query_vector.astype(jnp.float32).reshape(row_count, head_count, HEAD_WIDTH), lengths_here
    ).astype(jnp.bfloat16)
    new_keys = rotate(
        keyval[:, :kv_width].astype(jnp.float32).reshape(row_count, KV_HEADS, HEAD_WIDTH),
        lengths_here,
    ).astype(jnp.bfloat16)
    new_values = keyval[:, kv_width:].reshape(row_count, KV_HEADS, HEAD_WIDTH)
    grouped = queries.reshape(row_count, KV_HEADS, group_size, HEAD_WIDTH)
    old_keys = cached_key_rows.reshape(row_count, -1, KV_HEADS, HEAD_WIDTH)
    old_values = cached_value_rows.reshape(row_count, -1, KV_HEADS, HEAD_WIDTH)
    factor = 1.0 / math.sqrt(HEAD_WIDTH)
    scores = (
        jnp.einsum("rgqd,rcgd->rgqc", grouped, old_keys, preferred_element_type=jnp.float32)
        * factor
    )
    own_score = (
        jnp.einsum("rgqd,rgd->rgq", grouped, new_keys, preferred_element_type=jnp.float32) * factor
    )
    valid = jnp.arange(old_keys.shape[1], dtype=jnp.int32)[None, :] < lengths_here[:, None]
    scores = jnp.where(valid[:, None, None, :], scores, -jnp.inf)
    highest = jnp.maximum(jnp.max(scores, axis=-1), own_score)
    expos = jnp.exp(scores - highest[..., None])
    own_expo = jnp.exp(own_score - highest)
    total = jnp.sum(expos, axis=-1) + own_expo
    weights = (expos / total[..., None]).astype(jnp.bfloat16)
    own_weight = (own_expo / total).astype(jnp.bfloat16)
    context = jnp.einsum("rgqc,rcgd->rgqd", weights, old_values, preferred_element_type=jnp.float32)
    context = (
        context
        + own_weight.astype(jnp.float32)[..., None] * new_values.astype(jnp.float32)[:, :, None, :]
    )
    return context.reshape(row_count, head_count * HEAD_WIDTH)


def on_device(
    tokens,
    norm_gain_vector,
    query_weight,
    key_value_weight,
    output_weight,
    adapter_down_factor,
    adapter_up_factor,
    cached_key_rows,
    cached_value_rows,
    row_adapter_index,
    cached_length_rows,
    adapter_slot_index,
):
    position = lax.axis_index("tp")
    tp = lax.axis_size("tp")
    adapter_count = adapter_slot_index.shape[0]
    resident_count = adapter_down_factor.shape[0]
    rank_width = adapter_down_factor.shape[2]
    hidden_width = adapter_down_factor.shape[1]
    table = row_adapter_index[:, None] == jnp.arange(adapter_count, dtype=jnp.int32)[None, :]
    slot = jnp.sum(jnp.where(table, adapter_slot_index[None, :], 0), axis=1)
    local_slots = position * resident_count + jnp.arange(resident_count, dtype=jnp.int32)
    owned = slot[:, None] == local_slots[None, :]
    down_factor_rows = jnp.transpose(adapter_down_factor, (1, 0, 2)).reshape(
        hidden_width, resident_count * rank_width
    )
    query_cols = query_weight.shape[1]
    kv_cols = key_value_weight.shape[1]
    piece = normalize_and_gather(tokens, norm_gain_vector, tp)
    piece_rows = piece.shape[0]
    query_part = jnp.dot(piece, query_weight, preferred_element_type=jnp.float32)
    kv_part = jnp.dot(piece, key_value_weight, preferred_element_type=jnp.float32)
    low_part = jnp.dot(piece, down_factor_rows, preferred_element_type=jnp.float32).reshape(
        piece_rows, resident_count, rank_width
    )
    low = low_part.astype(jnp.bfloat16)
    masked_low = jnp.where(owned[:, :, None], low, jnp.zeros((), jnp.bfloat16)).reshape(
        piece_rows, resident_count * rank_width
    )
    up_factor_rows = adapter_up_factor.reshape(
        resident_count * rank_width, adapter_up_factor.shape[2]
    )
    terms = jnp.dot(masked_low, up_factor_rows, preferred_element_type=jnp.float32)
    packed = jnp.concatenate([query_part, kv_part, terms], axis=1)
    packed = packed.reshape(tp, piece_rows // tp, packed.shape[1])
    received = exchange(packed, tp)
    own_rows = piece_rows // tp
    plain_query = jnp.transpose(received[:, :, :query_cols], (1, 0, 2)).reshape(own_rows, -1)
    row_keyval = (
        jnp.transpose(received[:, :, query_cols : query_cols + kv_cols], (1, 0, 2))
        .reshape(own_rows, -1)
    )
    row_keyval = lax.reduce_precision(row_keyval, 8, 7).astype(jnp.bfloat16)
    correction = jnp.sum(received[:, :, query_cols + kv_cols :], axis=0)
    row_query = lax.reduce_precision(plain_query + ADAPTER_SCALE * correction, 8, 7).astype(
        jnp.bfloat16
    )
    context = attend(row_query, row_keyval, cached_key_rows, cached_value_rows, cached_length_rows)
    heads = jnp.transpose(context.reshape(own_rows, tp, -1), (1, 0, 2))
    return project_and_scatter(heads, output_weight, tp)


def solution(mesh):
    in_specs = (
        P(("groups", "tp"), None),
        P(),
        P(None, "tp"),
        P(None, "tp"),
        P("tp", None),
        P(("groups", "tp"), None, None),
        P(("groups", "tp"), None, None),
        P(("groups", "tp"), None, None),
        P(("groups", "tp"), None, None),
        P("groups"),
        P(("groups", "tp")),
        P("groups"),
    )
    out_specs = P(("groups", "tp"), None)
    return jax.shard_map(
        on_device, mesh=mesh, in_specs=in_specs, out_specs=out_specs, check_vma=False
    )
```
